128 devices in a mesh: dp: 4 (over y_lo, core), expert: 32 (over x, z, y_hi).
Axes of the slice: x: 4, y: 4 (y_hi: 2, y_lo: 2; y = y_hi * 2 + y_lo), z: 4, core: 2. Of those that a mesh axis runs over, the one named last changes fastest.
Arguments:
- tokens: bfloat16 [32768, 1440], P(('dp', 'expert')), may hold values from -6 to 6
- d_out: bfloat16 [32768, 1440], P(('dp', 'expert')), may hold values from -6 to 6
- route_ids: int32 [32768, 4], P(('dp', 'expert')), may hold values from 0 to 127, all different within a row; in each aligned block of 256 rows (0 to 255, 256 to 511, ...) at most 24 rows name the same one
- route_probs: float32 [32768, 4], P(('dp', 'expert')), may hold values from 0.05 to 0.5
- w_gate_up: bfloat16 [32, 1440, 2880], P('expert'), may hold values from -0.15625 to 0.15625
- gate_up_bias: float32 [32, 2880], P('expert'), may hold values from -3 to 3
- w_down: bfloat16 [32, 1440, 1440], P('expert'), may hold values from -0.15625 to 0.15625
Outputs:
- d_tokens: bfloat16 [32768, 1440], P(('dp', 'expert'))
- d_w_gate_up: bfloat16 [32, 1440, 2880], P('expert', 'dp')
- d_w_down: bfloat16 [32, 1440, 1440], P('expert', 'dp')
The draws below stay inside these ranges and needn't reach their ends.
Inputs may be any that keep to these rules, and one draw needn't show every extreme that they name: `route_ids`: each row names 4 different experts; among the rows of one device no expert is named more than 24 times.
All inputs are finite; a program needn't handle non-finite values.
Results may differ from the reference program's by a relative error of at most 0.0059.
Values may be sent and summed in bfloat16 or wider, within the bound.
A program may use at most 192 MiB of HBM per device.

```python
import math
import jax
import jax.numpy as jnp
import numpy as np
from jax import lax

D = 1440
FF = 1440
TOP = 4
TOK_DEV = 256
TOKENS = 32768
EXPERTS = 32
ALL_EXPERTS = 128
CAP = 24
N_DP = 4
N_EXPERT = 32


def level_of(stream_key, extent, shards, smallest, top_value):
    gain = 1.0
    for dim, parts in shards:
        heights = jax.random.uniform(jax.random.fold_in(jax.random.fold_in(stream_key, 6), dim), (parts,), jnp.float32, smallest / len(shards), top_value / len(shards))
        gain = gain * jnp.repeat(jnp.exp(heights), extent[dim] // parts).reshape((-1,) + (1,) * (len(extent) - 1 - dim))
    return gain


def deal_out(rng, own, number, rows, amount, top, most, skew):
    order = jax.random.permutation(rng, amount)
    packed, common = shares(amount, rows * top, most, skew, True), shares(amount, rows * top, most, skew, False)
    places = jnp.arange(amount)

    def named(sizes, turn):
        used = int((sizes > 0).sum())
        fixed = max(1, used // 4)
        shifted = fixed + (places - fixed + turn * (used - fixed)) % max(1, amount - fixed)
        return jnp.zeros((amount,), jnp.int32).at[order[jnp.where(places < fixed, places, shifted)]].set(jnp.asarray(sizes, jnp.int32))

    sizes = jnp.where(number % 4 == 0, named(packed, number // 4), named(common, number - number // 4 - 1))
    mixed = jax.random.permutation(jax.random.fold_in(own, 3), amount)
    donor, taker = mixed[0:amount // 2 * 2:2], mixed[1:amount // 2 * 2:2]
    room = jnp.minimum(sizes[donor] - 1, most - sizes[taker]) // 2
    room = jnp.where((donor == order[0]) | (taker == order[0]) | (sizes[taker] == 0), 0, jnp.maximum(room, 0))
    shifted = jax.random.randint(jax.random.fold_in(own, 4), (amount // 2,), 0, 1 << 20) % (room + 1)
    sizes = sizes.at[donor].add(-shifted).at[taker].add(shifted)
    items = jnp.searchsorted(jnp.cumsum(sizes), jnp.arange(rows * top), side="right").astype(jnp.int32)
    listing = items.reshape(top, rows).T
    listing = listing[jax.random.permutation(jax.random.fold_in(own, 1), rows)]
    turn = jax.random.randint(jax.random.fold_in(own, 2), (rows, 1), 0, top)
    return jnp.take_along_axis(listing, (jnp.arange(top)[None, :] + turn) % top, axis=1)


def shares(amount, total, most, skew, full):
    portions = [(1 << 20) // math.isqrt(grade ** skew) + 1 for grade in range(1, amount + 1)]
    largest = most if full else min(most, max(-(-total // amount), total * portions[0] // sum(portions)))
    least = 1 if total - largest >= amount - 1 else 0
    given, spare = [largest] + [least] * (amount - 1), total - largest - least * (amount - 1)
    while spare > 0:
        candidates = [i for i in range(1, amount) if given[i] < largest] or [i for i in range(1, amount) if given[i] < most]
        pool, left = sum([portions[i] for i in candidates]), spare
        for i in candidates:
            addition = min(most - given[i], max(1, left * portions[i] // pool), spare)
            given[i] = given[i] + addition
            spare = spare - addition
    return np.array(given)


def bell_draw(rng, extent, spread, most, shards=(), kind=jnp.bfloat16):
    entries = spread * jax.random.normal(rng, extent, jnp.float32)
    if shards:
        entries = entries * level_of(rng, extent, shards, -0.22, 0.18)
    return jnp.clip(entries, -most, most).astype(kind)


def setup_inputs(seed: int = 0) -> dict:
    streams_of = jax.random.split(jax.random.key(seed), 8)
    tokens = bell_draw(streams_of[0], (TOKENS, D), 1.0, 6.0, ((0, 128),))
    d_out = bell_draw(streams_of[1], (TOKENS, D), 1.0, 6.0, ((0, 128),))
    route_ids_keys = jax.random.split(jax.random.fold_in(streams_of[2], 1), TOKENS // TOK_DEV)
    route_ids_turns = jax.random.permutation(jax.random.fold_in(streams_of[2], 3), TOKENS // TOK_DEV)
    route_ids = jax.vmap(lambda own, number: deal_out(jax.random.fold_in(streams_of[2], 2), own, number, TOK_DEV, ALL_EXPERTS, TOP, CAP, 2))(route_ids_keys, route_ids_turns).reshape((TOKENS, TOP))
    route_probs = jnp.clip(0.05 + 0.45 * jax.random.uniform(streams_of[3], (TOKENS, TOP), jnp.float32) ** level_of(streams_of[3], (TOKENS, TOP), ((0, 128),), -0.2, 0.2), 0.05, 0.5)
    w_gate_up = bell_draw(streams_of[4], (EXPERTS, D, 2 * FF), D ** -0.5, 0.15625, ((0, 32),))
    gate_up_bias = bell_draw(streams_of[5], (EXPERTS, 2 * FF), 0.5, 3.0, ((0, 32),), jnp.float32)
    w_down = bell_draw(streams_of[6], (EXPERTS, FF, D), FF ** -0.5, 0.15625, ((0, 32),))
    return dict(tokens=tokens, d_out=d_out, route_ids=route_ids, route_probs=route_probs, w_gate_up=w_gate_up, gate_up_bias=gate_up_bias, w_down=w_down)


def expert_pass(rows, scaled, w_gu, bias, w_dn):
    pre = jnp.dot(rows, w_gu, preferred_element_type=jnp.float32) + bias[None, :]
    gate = pre[:, :FF]
    upper = pre[:, FF:]
    sig = jax.nn.sigmoid(1.702 * gate)
    glu = gate * sig
    hidden = ((upper + 1.0) * glu).astype(jnp.bfloat16)
    d_hidden = jnp.dot(scaled, w_dn.T, preferred_element_type=jnp.float32)
    d_gate = d_hidden * (upper + 1.0) * (sig + 1.702 * gate * sig * (1.0 - sig))
    d_upper = d_hidden * glu
    d_pre = jnp.concatenate([d_gate, d_upper], axis=1).astype(jnp.bfloat16)
    d_route = jnp.dot(d_pre, w_gu.T, preferred_element_type=jnp.float32).astype(jnp.bfloat16)
    grad_gu = jnp.dot(rows.T, d_pre, preferred_element_type=jnp.float32).astype(jnp.bfloat16)
    grad_dn = jnp.dot(hidden.T, scaled, preferred_element_type=jnp.float32).astype(jnp.bfloat16)
    return d_route, grad_gu, grad_dn


def reference(tokens, d_out, route_ids, route_probs, w_gate_up, gate_up_bias, w_down):
    total_routes = TOKENS * TOP
    limit = N_DP * N_EXPERT * CAP
    route_list = route_ids.reshape(-1).astype(jnp.int32)
    route_rows = jnp.repeat(tokens, TOP, axis=0)
    scaled = (route_probs[:, :, None] * d_out[:, None, :].astype(jnp.float32)).astype(jnp.bfloat16).reshape(total_routes, D)
    rows_padded = jnp.concatenate([route_rows, jnp.zeros((1, D), jnp.bfloat16)], axis=0)
    scaled_padded = jnp.concatenate([scaled, jnp.zeros((1, D), jnp.bfloat16)], axis=0)

    def one_expert(number):
        picked = jnp.nonzero(route_list == number, size=limit, fill_value=total_routes)[0].astype(jnp.int32)
        d_route, grad_gu, grad_dn = expert_pass(rows_padded[picked], scaled_padded[picked], w_gate_up[number], gate_up_bias[number], w_down[number])
        return picked, d_route, grad_gu, grad_dn

    picked, d_route, grad_gu, grad_dn = lax.map(one_expert, jnp.arange(EXPERTS, dtype=jnp.int32))
    collected = jnp.zeros((total_routes + 1, D), jnp.float32).at[picked.reshape(-1)].set(d_route.reshape(-1, D).astype(jnp.float32))
    d_tokens = jnp.sum(collected[:total_routes].reshape(TOKENS, TOP, D), axis=1).astype(jnp.bfloat16)
    return d_tokens, grad_gu, grad_dn
```

```python
import jax
import jax.numpy as jnp
from jax import lax
from jax.experimental import pallas as pl
from jax.experimental.pallas import tpu as pltpu
from jax.sharding import PartitionSpec as P

MESH = pl.DeviceIdType.MESH
F32 = jnp.float32
BF16 = jnp.bfloat16
OWNERS = 32
CAP = 24
WIDTH = 1440
HALF = 720
SHARD = 360
PAD = 1536
TILE = 512
GROUP = 8
ROWS = GROUP * CAP


def nt(a, b):
    return lax.dot_general(a, b, (((1,), (1,)), ((), ())), preferred_element_type=F32)


def tn(a, b):
    return lax.dot_general(a, b, (((0,), (0,)), ((), ())), preferred_element_type=F32)


def nn(a, b):
    return jnp.dot(a, b, preferred_element_type=F32)


def route_kernel(ids_ref, probs_ref, tok_ref, dout_ref, rows_ref, scaled_ref, pick_ref):
    me = lax.axis_index("expert")
    toks = ids_ref.shape[1]
    r = lax.broadcasted_iota(jnp.int32, (OWNERS, toks), 0)
    i = (r >> 1) & 3
    x = ((me >> 3) + i) & 3
    z = ((me >> 1) + (r >> 3) - i) & 3
    expert = x * 8 + z * 2 + ((me ^ r) & 1)
    named = jnp.zeros((OWNERS, toks), F32)
    prob = jnp.zeros((OWNERS, toks), F32)
    for k in range(ids_ref.shape[0]):
        hit = ids_ref[k : k + 1, :] == expert
        named = named + jnp.where(hit, 1.0, 0.0)
        prob = prob + jnp.where(hit, probs_ref[k : k + 1, :], 0.0)
    before = lax.broadcasted_iota(jnp.int32, (toks, toks), 0) < lax.broadcasted_iota(
        jnp.int32, (toks, toks), 1
    )
    rank = nn(named.astype(BF16), jnp.where(before, 1.0, 0.0).astype(BF16))
    code = jnp.where(named > 0.0, rank, -1.0)
    step = 8
    for g in range(OWNERS // step):
        part = slice(step * g, step * g + step)
        lines = slice(step * CAP * g, step * CAP * (g + 1))
        place = lax.broadcasted_iota(jnp.int32, (step, CAP, toks), 1).astype(F32)
        pick = jnp.broadcast_to(code[part][:, None, :], (step, CAP, toks)) == place
        pick = pick.reshape(step * CAP, toks) if False else pick
        ones = jnp.where(pick, 1.0, 0.0)
        weight = jnp.sum(
            jnp.where(pick, jnp.broadcast_to(prob[part][:, None, :], (step, CAP, toks)), 0.0),
            axis=2,
            keepdims=True,
        ).reshape(step * CAP, 1)
        ones = ones.reshape(step * CAP, toks).astype(BF16)
        pick_ref[lines, :] = ones
        rows_ref[lines, :] = nn(ones, tok_ref[...]).astype(BF16)
        scaled_ref[lines, :] = (nn(ones, dout_ref[...]) * weight).astype(BF16)


def combine_kernel(pick_ref, back_ref, out_ref):
    out_ref[...] = tn(pick_ref[...], back_ref[...]).astype(BF16)


def main_kernel(
    bias_ref,
    rows_ref,
    scaled_ref,
    wgu_ref,
    wdn_ref,
    out_gu_ref,
    out_dn_ref,
    back_ref,
    got_rows,
    got_scaled,
    wgu,
    wu,
    wdn,
    acc,
    dgate,
    dup,
    hid,
    rows_t,
    hid_t,
    droute,
    give,
    take,
    w_sem,
    send_sem,
    recv_sem,
    fwd_send,
    fwd_recv,
    back_send,
    back_recv,
    self_sem,
    core_send,
    core_recv,
):
    dp = lax.axis_index("dp")
    me = lax.axis_index("expert")
    l = dp // 2
    c = dp % 2
    mx, mz, mh = me // 8, (me // 2) % 4, me % 2

    def target(r, sign):
        k, i, low = r // 8, (r // 2) % 4, r % 2
        x = (mx + sign * i + 4) % 4
        z = (mz + sign * (k - i) + 8) % 4
        h = (mh + low) % 2
        return (((l + low) % 2) * 2 + c, x * 8 + z * 2 + h)

    over_y = ((1 - l) * 2 + c, me)
    over_core = (l * 2 + 1 - c, me)

    load_gu = pltpu.make_async_copy(wgu_ref.at[0], wgu, w_sem.at[0])
    load_dn = pltpu.make_async_copy(wdn_ref.at[0], wdn.at[pl.ds(0, WIDTH)], w_sem.at[1])
    load_gu.start()
    load_dn.start()

    barrier = pltpu.get_barrier_semaphore()

    def greet(r, _):
        pl.semaphore_signal(barrier, inc=1, device_id=target(r, 1), device_id_type=MESH)
        return 0

    lax.fori_loop(1, OWNERS, greet, 0)
    pl.semaphore_signal(barrier, inc=1, device_id=over_y, device_id_type=MESH)
    pl.semaphore_signal(barrier, inc=1, device_id=over_core, device_id_type=MESH)
    pl.semaphore_wait(barrier, OWNERS + 1)

    def slot(ref, region, r):
        return ref.at[region, r // 4, r % 4]

    for n, (src, dst) in enumerate(((rows_ref, got_rows), (scaled_ref, got_scaled))):
        pltpu.make_async_copy(src.at[0], dst.at[0, 0, 0], recv_sem.at[0, n]).start()

    def dispatch(r, _):
        for n, (src, dst) in enumerate(((rows_ref, got_rows), (scaled_ref, got_scaled))):
            pltpu.make_async_remote_copy(
                src_ref=src.at[r],
                dst_ref=slot(dst, 0, r),
                send_sem=send_sem.at[n],
                recv_sem=recv_sem.at[r // 4, n],
                device_id=target(r, 1),
                device_id_type=MESH,
            ).start()
        return 0

    lax.fori_loop(1, OWNERS, dispatch, 0)

    def forward(p, n):
        buf = (got_rows, got_scaled)[n]
        return pltpu.make_async_remote_copy(
            src_ref=buf.at[0, p],
            dst_ref=buf.at[1, p],
            send_sem=fwd_send.at[p, n],
            recv_sem=fwd_recv.at[p, n],
            device_id=over_y,
            device_id_type=MESH,
        )

    def relay(p, _):
        for n, buf in enumerate((got_rows, got_scaled)):
            pltpu.make_async_copy(buf.at[0, p], buf.at[0, p], recv_sem.at[p, n]).wait()
            forward(p, n).start()
        return 0

    lax.fori_loop(0, 2, relay, 0)

    load_gu.wait()
    load_dn.wait()
    wdn[WIDTH:PAD, :] = jnp.zeros((PAD - WIDTH, WIDTH), BF16)
    wu[:, WIDTH:PAD] = jnp.zeros((WIDTH, PAD - WIDTH), BF16)

    def shift(q, _):
        lines = pl.ds(pl.multiple_of(q * 144, 16), 144)
        wu[lines, 0:WIDTH] = wgu[lines, WIDTH : 2 * WIDTH]
        return 0

    lax.fori_loop(0, 10, shift, 0)
    acc[...] = jnp.zeros_like(acc)

    def inner(region, j):
        lines = slice(region * ROWS, (region + 1) * ROWS)
        x = got_rows[region, pl.ds(2 * j, 2)].reshape(ROWS, WIDTH)
        y = got_scaled[region, pl.ds(2 * j, 2)].reshape(ROWS, WIDTH)
        for t in range(PAD // TILE):
            cols = slice(t * TILE, (t + 1) * TILE)
            bias_u = bias_ref[:, WIDTH + t * TILE : min(WIDTH + (t + 1) * TILE, 2 * WIDTH)]
            if bias_u.shape[1] < TILE:
                bias_u = jnp.concatenate(
                    [bias_u, jnp.zeros((1, TILE - bias_u.shape[1]), F32)], axis=1
                )
            g = nn(x, wgu[:, cols]) + bias_ref[:, cols]
            u = nn(x, wu[:, cols]) + bias_u + 1.0
            dh = nt(y, wdn[cols, :])
            s = jax.nn.sigmoid(1.702 * g)
            glu = g * s
            hid[lines, cols] = (u * glu).astype(BF16)
            dup[lines, cols] = (dh * glu).astype(BF16)
            dgate[lines, cols] = (dh * u * (s + 1.702 * glu * (1.0 - s))).astype(BF16)

    def back_copy(r):
        return pltpu.make_async_remote_copy(
            src_ref=droute.at[r],
            dst_ref=back_ref.at[r],
            send_sem=back_send,
            recv_sem=back_recv,
            device_id=target(r, -1),
            device_id_type=MESH,
        )

    own_back = pltpu.make_async_copy(droute.at[0], back_ref.at[0], self_sem)

    def superstep(j, _):
        @pl.when(j < 3)
        def _():
            lax.fori_loop(2 * j + 2, 2 * j + 4, relay, 0)

        inner(0, j)
        for first in range(0, WIDTH, TILE):
            cols = slice(first, min(first + TILE, WIDTH))
            part = nt(dgate[0:ROWS, :], wgu[cols, 0:PAD]) + nt(dup[0:ROWS, :], wu[cols, :])
            part = part.reshape(GROUP, CAP, cols.stop - cols.start).astype(BF16)
            droute[pl.ds(GROUP * j, GROUP), :, cols] = part

        def send_back(r, _):
            @pl.when(r == 0)
            def _():
                own_back.start()

            @pl.when(r > 0)
            def _():
                back_copy(r).start()

            return 0

        lax.fori_loop(GROUP * j, GROUP * j + GROUP, send_back, 0)

        def arrive(p, _):
            for n in range(2):
                forward(p, n).wait_recv()
            return 0

        lax.fori_loop(2 * j, 2 * j + 2, arrive, 0)
        inner(1, j)
        x = got_rows[:, pl.ds(2 * j, 2)].reshape(2 * ROWS, WIDTH)
        y = got_scaled[:, pl.ds(2 * j, 2)].reshape(2 * ROWS, WIDTH)
        for side in range(2):

            @pl.when(l == side)
            def _():
                cols = slice(HALF * side, HALF * (side + 1))
                rows_t[...] = x[:, cols].T
                hid_t[...] = hid[:, cols].T

        for t in range(PAD // TILE):
            cols = slice(t * TILE, (t + 1) * TILE)
            acc[0, :, cols] += nn(rows_t[...], dgate[:, cols])
            acc[1, :, cols] += nn(rows_t[...], dup[:, cols])
            cols = slice(t * TILE, min((t + 1) * TILE, WIDTH))
            acc[2, :, cols] += nn(hid_t[...], y[:, cols])
        return 0

    lax.fori_loop(0, 4, superstep, 0)

    def core_copy(n):
        return pltpu.make_async_remote_copy(
            src_ref=give.at[n],
            dst_ref=take.at[n],
            send_sem=core_send.at[n],
            recv_sem=core_recv.at[n],
            device_id=over_core,
            device_id_type=MESH,
        )

    other = pl.ds(pl.multiple_of((1 - c) * SHARD, 8), SHARD)
    mine = pl.ds(pl.multiple_of(c * SHARD, 8), SHARD)
    for n in range(3):
        give[n] = acc[n, other, 0:WIDTH].astype(BF16)
        core_copy(n).start()
    outs = (out_gu_ref.at[:, 0:WIDTH], out_gu_ref.at[:, WIDTH : 2 * WIDTH], out_dn_ref)
    for n in range(3):
        core_copy(n).wait_recv()
        total = (acc[n, mine, 0:WIDTH] + take[n].astype(F32)).astype(BF16)
        if n == 0:
            out_gu_ref[:, 0:WIDTH] = total
        elif n == 1:
            out_gu_ref[:, WIDTH : 2 * WIDTH] = total
        else:
            out_dn_ref[...] = total

    for n in range(3):
        core_copy(n).wait_send()
    for n, src in enumerate((rows_ref, scaled_ref)):
        some = src.at[pl.ds(1, OWNERS - 1)]
        pltpu.make_async_copy(some, some, send_sem.at[n]).wait()

    def settle(p, _):
        for n in range(2):
            forward(p, n).wait_send()
        return 0

    lax.fori_loop(0, 8, settle, 0)
    some = droute.at[pl.ds(1, OWNERS - 1)]
    pltpu.make_async_copy(some, some, back_send).wait()
    some = back_ref.at[pl.ds(1, OWNERS - 1)]
    pltpu.make_async_copy(some, some, back_recv).wait()
    own_back.wait()


def shards(tokens, d_out, route_ids, route_probs, w_gate_up, gate_up_bias, w_down):
    toks = tokens.shape[0]
    vmem = pl.BlockSpec(memory_space=pltpu.VMEM)
    hbm = pl.BlockSpec(memory_space=pl.ANY)
    slots = OWNERS * CAP
    rows, scaled, pick = pl.pallas_call(
        route_kernel,
        name="route",
        out_shape=(
            jax.ShapeDtypeStruct((slots, WIDTH), BF16),
            jax.ShapeDtypeStruct((slots, WIDTH), BF16),
            jax.ShapeDtypeStruct((slots, toks), BF16),
        ),
        in_specs=[vmem] * 4,
        out_specs=(vmem, vmem, vmem),
        compiler_params=pltpu.CompilerParams(vmem_limit_bytes=40 * 2**20),
    )(route_ids.T, route_probs.T, tokens, d_out)
    blocks = (OWNERS, CAP, WIDTH)
    grad_gu, grad_dn, back = pl.pallas_call(
        main_kernel,
        name="experts",
        out_shape=(
            jax.ShapeDtypeStruct((SHARD, 2 * WIDTH), BF16),
            jax.ShapeDtypeStruct((SHARD, WIDTH), BF16),
            jax.ShapeDtypeStruct(blocks, BF16),
        ),
        in_specs=[vmem, hbm, hbm, hbm, hbm],
        out_specs=(vmem, vmem, hbm),
        scratch_shapes=[
            pltpu.VMEM((2, 8, 4, CAP, WIDTH), BF16),
            pltpu.VMEM((2, 8, 4, CAP, WIDTH), BF16),
            pltpu.VMEM((WIDTH, 2 * WIDTH), BF16),
            pltpu.VMEM((WIDTH, PAD), BF16),
            pltpu.VMEM((PAD, WIDTH), BF16),
            pltpu.VMEM((3, HALF, PAD), F32),
            pltpu.VMEM((2 * ROWS, PAD), BF16),
            pltpu.VMEM((2 * ROWS, PAD), BF16),
            pltpu.VMEM((2 * ROWS, PAD), BF16),
            pltpu.VMEM((HALF, 2 * ROWS), BF16),
            pltpu.VMEM((HALF, 2 * ROWS), BF16),
            pltpu.VMEM(blocks, BF16),
            pltpu.VMEM((3, SHARD, WIDTH), BF16),
            pltpu.VMEM((3, SHARD, WIDTH), BF16),
            pltpu.SemaphoreType.DMA((2,)),
            pltpu.SemaphoreType.DMA((2,)),
            pltpu.SemaphoreType.DMA((8, 2)),
            pltpu.SemaphoreType.DMA((8, 2)),
            pltpu.SemaphoreType.DMA((8, 2)),
            pltpu.SemaphoreType.DMA,
            pltpu.SemaphoreType.DMA,
            pltpu.SemaphoreType.DMA,
            pltpu.SemaphoreType.DMA((3,)),
            pltpu.SemaphoreType.DMA((3,)),
        ],
        compiler_params=pltpu.CompilerParams(
            collective_id=0, has_side_effects=True, vmem_limit_bytes=63 * 2**20
        ),
    )(gate_up_bias, rows.reshape(blocks), scaled.reshape(blocks), w_gate_up, w_down)
    d_tokens = pl.pallas_call(
        combine_kernel,
        name="combine",
        out_shape=jax.ShapeDtypeStruct((toks, WIDTH), BF16),
        in_specs=[vmem, vmem],
        out_specs=vmem,
        compiler_params=pltpu.CompilerParams(vmem_limit_bytes=40 * 2**20),
    )(pick, back.reshape(slots, WIDTH))
    return d_tokens, grad_gu[None], grad_dn[None]


def solution(mesh):
    in_specs = (
        P(("dp", "expert"), None),
        P(("dp", "expert"), None),
        P(("dp", "expert"), None),
        P(("dp", "expert"), None),
        P("expert", None, None),
        P("expert", None),
        P("expert", None, None),
    )
    out_specs = (P(("dp", "expert"), None), P("expert", "dp", None), P("expert", "dp", None))
    return jax.shard_map(shards, mesh=mesh, in_specs=in_specs, out_specs=out_specs, check_vma=False)
```

```python
import jax
import jax.numpy as jnp
from jax import lax
from jax.experimental import pallas as pl
from jax.experimental.pallas import tpu as pltpu
from jax.sharding import PartitionSpec as P

MESH = pl.DeviceIdType.MESH
F32 = jnp.float32
BF16 = jnp.bfloat16
OWNERS = 32
CAP = 24
WIDTH = 1440
MAIN = 1408
HALF = 720
SHARD = 360
LINES = 368
PAD = 1536
TILE = 512
GROUP = 8
ROWS = GROUP * CAP


def nt(a, b):
    return lax.dot_general(a, b, (((1,), (1,)), ((), ())), preferred_element_type=F32)


def tn(a, b):
    return lax.dot_general(a, b, (((0,), (0,)), ((), ())), preferred_element_type=F32)


def nn(a, b):
    return jnp.dot(a, b, preferred_element_type=F32)


def finish_kernel(
    pick_ref, back_ref, gu_ref, dn_ref, tok_ref, out_gu_ref, out_dn_ref, pick, back, gu, dn, sem
):
    ins = [
        pltpu.make_async_copy(src, dst, sem.at[n])
        for n, (src, dst) in enumerate(
            ((back_ref, back), (pick_ref, pick), (dn_ref, dn), (gu_ref, gu))
        )
    ]
    outs = [
        pltpu.make_async_copy(dn, out_dn_ref, sem.at[4]),
        pltpu.make_async_copy(gu, out_gu_ref, sem.at[5]),
    ]
    for copy in ins:
        copy.start()
    for n in range(2):
        ins[2 + n].wait()
        outs[n].start()
    ins[0].wait()
    ins[1].wait()
    tok_ref[...] = tn(pick[...], back[:, 0:WIDTH]).astype(BF16).T
    for copy in outs:
        copy.wait()


def main_kernel(
    ids_ref,
    probs_ref,
    bias_ref,
    tok_ref,
    dout_ref,
    wgu_ref,
    wdn_ref,
    pick_ref,
    out_gu_ref,
    out_dn_ref,
    back_ref,
    tok,
    dout,
    code,
    prob,
    send,
    got,
    rows,
    scaled,
    wgu,
    wu,
    wdn,
    acc,
    work,
    rows_t,
    hid_t,
    take,
    load_sem,
    send_sem,
    recv_sem,
    fwd_send,
    fwd_recv,
    back_send,
    back_recv,
    self_sem,
    core_send,
    core_recv,
):
    dp = lax.axis_index("dp")
    me = lax.axis_index("expert")
    l = dp // 2
    c = dp % 2
    mx, mz, mh = me // 8, (me // 2) % 4, me % 2

    def target(r, sign):
        k, i, low = r // 8, (r // 2) % 4, r % 2
        x = (mx + sign * i + 4) % 4
        z = (mz + sign * (k - i) + 8) % 4
        h = (mh + low) % 2
        return (((l + low) % 2) * 2 + c, x * 8 + z * 2 + h)

    over_y = ((1 - l) * 2 + c, me)
    over_core = (l * 2 + 1 - c, me)

    loads = [
        pltpu.make_async_copy(src, dst, load_sem.at[n])
        for n, (src, dst) in enumerate(
            (
                (tok_ref, tok),
                (dout_ref, dout),
                (wgu_ref.at[0], wgu),
                (wdn_ref.at[0], wdn.at[pl.ds(0, WIDTH)]),
            )
        )
    ]
    for load in loads[:2]:
        load.start()

    barrier = pltpu.get_barrier_semaphore()

    def greet(r, _):
        pl.semaphore_signal(barrier, inc=1, device_id=target(r, 1), device_id_type=MESH)
        return 0

    lax.fori_loop(1, OWNERS, greet, 0)
    pl.semaphore_signal(barrier, inc=1, device_id=over_y, device_id_type=MESH)
    pl.semaphore_signal(barrier, inc=1, device_id=over_core, device_id_type=MESH)

    toks = ids_ref.shape[1]
    r = lax.broadcasted_iota(jnp.int32, (OWNERS, toks), 0)
    i = (r >> 1) & 3
    x = ((me >> 3) + i) & 3
    z = ((me >> 1) + (r >> 3) - i) & 3
    expert = x * 8 + z * 2 + ((me ^ r) & 1)
    named = jnp.zeros((OWNERS, toks), F32)
    weight = jnp.zeros((OWNERS, toks), F32)
    for k in range(ids_ref.shape[0]):
        hit = ids_ref[k : k + 1, :] == expert
        named = named + jnp.where(hit, 1.0, 0.0)
        weight = weight + jnp.where(hit, probs_ref[k : k + 1, :], 0.0)
    before = lax.broadcasted_iota(jnp.int32, (toks, toks), 0) < lax.broadcasted_iota(
        jnp.int32, (toks, toks), 1
    )
    rank = nn(named.astype(BF16), jnp.where(before, 1.0, 0.0).astype(BF16))
    code[...] = jnp.where(named > 0.0, rank, -1.0)
    prob[...] = weight
    for load in loads[:2]:
        load.wait()
    for load in loads[2:]:
        load.start()

    def fill(g):
        part = pl.ds(pl.multiple_of(g * GROUP, GROUP), GROUP)
        place = lax.broadcasted_iota(jnp.int32, (GROUP, CAP, toks), 1).astype(F32)
        chosen = jnp.broadcast_to(code[part, :][:, None, :], place.shape) == place
        ones = jnp.where(chosen, 1.0, 0.0).reshape(ROWS, toks).astype(BF16)
        share = jnp.where(chosen, jnp.broadcast_to(prob[part, :][:, None, :], place.shape), 0.0)
        share = jnp.sum(share, axis=2, keepdims=True).reshape(ROWS, 1)
        pick_ref[pl.ds(pl.multiple_of(g * ROWS, ROWS), ROWS), :] = ones
        both = pl.ds(2 * g, 2)
        for n, src in enumerate((tok, dout)):
            value = nt(ones, src[...])
            if n == 1:
                value = value * share
            for first, last, where in (
                (0, MAIN, n * MAIN),
                (MAIN, WIDTH, 2 * MAIN + n * (WIDTH - MAIN)),
            ):
                piece = value[:, first:last].reshape(2, GROUP // 2, CAP, last - first)
                send[both, :, :, where : where + last - first] = piece.astype(BF16)

    def slot(region, r):
        return got.at[region, r // 4, r % 4]

    def relay_copy(src, dst, r, device):
        return pltpu.make_async_remote_copy(
            src_ref=src,
            dst_ref=dst,
            send_sem=fwd_send.at[r],
            recv_sem=fwd_recv.at[r],
            device_id=device,
            device_id_type=MESH,
        )

    def forward_block(r):
        return relay_copy(slot(0, r), slot(1, r), r, over_y)

    def dispatch(r, _):
        pltpu.make_async_remote_copy(
            src_ref=send.at[r // 4, r % 4],
            dst_ref=slot(0, r),
            send_sem=send_sem.at[r // 4],
            recv_sem=recv_sem.at[r],
            device_id=target(r, 1),
            device_id_type=MESH,
        ).start()
        return 0

    fill(0)
    pl.semaphore_wait(barrier, OWNERS + 1)
    own = pltpu.make_async_copy(send.at[0, 0], slot(0, 0), recv_sem.at[0])
    own.start()
    relay_copy(send.at[0, 0], slot(1, 0), 0, over_y).start()
    lax.fori_loop(1, GROUP, dispatch, 0)

    def fill_next(g, _):
        fill(g)
        lax.fori_loop(GROUP * g, GROUP * g + GROUP, dispatch, 0)
        return 0

    lax.fori_loop(1, OWNERS // GROUP, fill_next, 0)

    loads[2].wait()
    loads[3].wait()
    wdn[WIDTH:PAD, :] = jnp.zeros((PAD - WIDTH, WIDTH), BF16)
    wu[:, WIDTH:PAD] = jnp.zeros((WIDTH, PAD - WIDTH), BF16)

    def shift(q, _):
        lines = pl.ds(pl.multiple_of(q * 144, 16), 144)
        wu[lines, 0:WIDTH] = wgu[lines, WIDTH : 2 * WIDTH]
        return 0

    lax.fori_loop(0, 10, shift, 0)
    own.wait()

    def landed(r):
        pltpu.make_async_copy(slot(0, r), slot(0, r), recv_sem.at[r]).wait()

    def relay_block(r, _):
        landed(r)
        forward_block(r).start()
        return 0

    lax.fori_loop(1, GROUP, relay_block, 0)
    acc[...] = jnp.zeros_like(acc)

    def inner(region, j):
        lines = slice(region * ROWS, (region + 1) * ROWS)
        both = pl.ds(2 * j, 2)
        tail = 2 * MAIN
        more = WIDTH - MAIN
        for n, dst in enumerate((rows, scaled)):
            dst[lines, 0:MAIN] = got[region, both, :, :, n * MAIN : (n + 1) * MAIN].reshape(
                ROWS, MAIN
            )
        ends = got[region, both, :, :, tail : tail + 2 * more].reshape(ROWS, 2 * more)
        rows[lines, MAIN:WIDTH] = ends[:, 0:more]
        scaled[lines, MAIN:WIDTH] = ends[:, more:]
        for t in range(PAD // TILE):
            cols = slice(t * TILE, (t + 1) * TILE)
            bias_u = bias_ref[:, WIDTH + t * TILE : min(WIDTH + (t + 1) * TILE, 2 * WIDTH)]
            if bias_u.shape[1] < TILE:
                bias_u = jnp.concatenate(
                    [bias_u, jnp.zeros((1, TILE - bias_u.shape[1]), F32)], axis=1
                )
            g = nn(rows[lines, :], wgu[:, cols]) + bias_ref[:, cols]
            u = nn(rows[lines, :], wu[:, cols]) + bias_u + 1.0
            dh = nt(scaled[lines, :], wdn[cols, :])
            s = jax.nn.sigmoid(1.702 * g)
            glu = g * s
            work[2, lines, cols] = (u * glu).astype(BF16)
            work[1, lines, cols] = (dh * glu).astype(BF16)
            work[0, lines, cols] = (dh * u * (s + 1.702 * glu * (1.0 - s))).astype(BF16)

    def sent(p, count):
        some = send.at[p, pl.ds(4 - count, count)]
        pltpu.make_async_copy(some, some, send_sem.at[p]).wait()

    def back_copy(r):
        return pltpu.make_async_remote_copy(
            src_ref=send.at[r // 4, r % 4, :, pl.ds(0, PAD)],
            dst_ref=back_ref.at[r],
            send_sem=back_send,
            recv_sem=back_recv,
            device_id=target(r, -1),
            device_id_type=MESH,
        )

    own_back = pltpu.make_async_copy(
        send.at[0, 0, :, pl.ds(0, PAD)], back_ref.at[0], self_sem
    )

    def give_back(j):
        @pl.when(j == 0)
        def _():
            sent(0, 3)
            sent(1, 4)
            forward_block(0).wait_send()

        @pl.when(j > 0)
        def _():
            sent(2 * j, 4)
            sent(2 * j + 1, 4)

        for first in range(0, WIDTH, TILE):
            cols = slice(first, min(first + TILE, WIDTH))
            part = nt(work[0, 0:ROWS, :], wgu[cols, 0:PAD]) + nt(work[1, 0:ROWS, :], wu[cols, :])
            part = part.reshape(2, GROUP // 2, CAP, cols.stop - cols.start).astype(BF16)
            send[pl.ds(2 * j, 2), :, :, cols] = part

        def send_back(r, _):
            @pl.when(r == 0)
            def _():
                own_back.start()

            @pl.when(r > 0)
            def _():
                back_copy(r).start()

            return 0

        lax.fori_loop(GROUP * j, GROUP * j + GROUP, send_back, 0)

    def arrive(j):
        def one(r, _):
            forward_block(r).wait_recv()
            return 0

        lax.fori_loop(GROUP * j, GROUP * j + GROUP, one, 0)

    def turn(lines):
        at = slice(0, lines.stop - lines.start)
        for side in range(2):

            @pl.when(l == side)
            def _():
                cols = slice(HALF * side, HALF * (side + 1))
                rows_t[:, at] = rows[lines, cols].T
                hid_t[:, at] = work[2, lines, cols].T

    def add(n, lines):
        left = (rows_t, rows_t, hid_t)[n].at[:, 0 : lines.stop - lines.start]
        for t in range(PAD // TILE):
            cols = slice(t * TILE, (t + 1) * TILE)
            if n < 2:
                acc[n, :, cols] += nn(left[...], work[n, lines, cols])
            else:
                cols = slice(t * TILE, min((t + 1) * TILE, WIDTH))
                acc[n, :, cols] += nn(left[...], scaled[lines, cols])

    every = slice(0, 2 * ROWS)

    def superstep(j, _):
        lax.fori_loop(GROUP * (j + 1), GROUP * (j + 2), relay_block, 0)
        inner(0, j)
        give_back(j)
        arrive(j)
        inner(1, j)
        turn(every)
        for n in range(3):
            add(n, every)
        return 0

    lax.fori_loop(0, 3, superstep, 0)

    def core_copy(n):
        return pltpu.make_async_remote_copy(
            src_ref=work.at[n, pl.ds(0, LINES)],
            dst_ref=take.at[n],
            send_sem=core_send.at[n],
            recv_sem=core_recv.at[n],
            device_id=over_core,
            device_id_type=MESH,
        )

    inner(0, 3)
    give_back(3)
    turn(slice(0, ROWS))
    for n in range(3):
        add(n, slice(0, ROWS))
    arrive(3)
    late = slice(ROWS, 2 * ROWS)
    inner(1, 3)
    turn(late)
    other = pl.ds(pl.multiple_of((1 - c) * SHARD, 8), SHARD)
    mine = pl.ds(pl.multiple_of(c * SHARD, 8), SHARD)
    for n in range(3):
        add(n, late)
        work[n, 0:SHARD, 0:WIDTH] = acc[n, other, 0:WIDTH].astype(BF16)
        core_copy(n).start()
    for n in range(3):
        core_copy(n).wait_recv()
        total = (acc[n, mine, 0:WIDTH] + take[n, 0:SHARD, 0:WIDTH].astype(F32)).astype(BF16)
        if n < 2:
            out_gu_ref[:, n * WIDTH : (n + 1) * WIDTH] = total
        else:
            out_dn_ref[...] = total

    for n in range(3):
        core_copy(n).wait_send()

    def settle_block(r, _):
        forward_block(r).wait_send()
        return 0

    lax.fori_loop(1, OWNERS, settle_block, 0)
    some = back_ref.at[pl.ds(1, OWNERS - 1)]
    pltpu.make_async_copy(some, some, back_send).wait()
    pltpu.make_async_copy(some, some, back_recv).wait()
    own_back.wait()


def shards(tokens, d_out, route_ids, route_probs, w_gate_up, gate_up_bias, w_down):
    toks = tokens.shape[0]
    vmem = pl.BlockSpec(memory_space=pltpu.VMEM)
    hbm = pl.BlockSpec(memory_space=pl.ANY)
    slots = OWNERS * CAP
    block = (CAP, 2 * WIDTH)
    grads = (
        jax.ShapeDtypeStruct((SHARD, 2 * WIDTH), BF16),
        jax.ShapeDtypeStruct((SHARD, WIDTH), BF16),
    )
    pick, grad_gu, grad_dn, back = pl.pallas_call(
        main_kernel,
        name="experts",
        out_shape=(
            jax.ShapeDtypeStruct((slots, toks), BF16),
            *grads,
            jax.ShapeDtypeStruct((OWNERS, CAP, PAD), BF16),
        ),
        in_specs=[vmem] * 3 + [hbm] * 4,
        out_specs=(vmem, vmem, vmem, hbm),
        scratch_shapes=[
            pltpu.VMEM((WIDTH, toks), BF16),
            pltpu.VMEM((WIDTH, toks), BF16),
            pltpu.VMEM((OWNERS, toks), F32),
            pltpu.VMEM((OWNERS, toks), F32),
            pltpu.VMEM((8, 4, *block), BF16),
            pltpu.VMEM((2, 8, 4, *block), BF16),
            pltpu.VMEM((2 * ROWS, WIDTH), BF16),
            pltpu.VMEM((2 * ROWS, WIDTH), BF16),
            pltpu.VMEM((WIDTH, 2 * WIDTH), BF16),
            pltpu.VMEM((WIDTH, PAD), BF16),
            pltpu.VMEM((PAD, WIDTH), BF16),
            pltpu.VMEM((3, HALF, PAD), F32),
            pltpu.VMEM((3, 2 * ROWS, PAD), BF16),
            pltpu.VMEM((HALF, 2 * ROWS), BF16),
            pltpu.VMEM((HALF, 2 * ROWS), BF16),
            pltpu.VMEM((3, LINES, PAD), BF16),
            pltpu.SemaphoreType.DMA((4,)),
            pltpu.SemaphoreType.DMA((8,)),
            pltpu.SemaphoreType.DMA((OWNERS,)),
            pltpu.SemaphoreType.DMA((OWNERS,)),
            pltpu.SemaphoreType.DMA((OWNERS,)),
            pltpu.SemaphoreType.DMA,
            pltpu.SemaphoreType.DMA,
            pltpu.SemaphoreType.DMA,
            pltpu.SemaphoreType.DMA((3,)),
            pltpu.SemaphoreType.DMA((3,)),
        ],
        compiler_params=pltpu.CompilerParams(
            collective_id=0, has_side_effects=True, vmem_limit_bytes=63 * 2**20
        ),
    )(route_ids.T, route_probs.T, gate_up_bias, tokens.T, d_out.T, w_gate_up, w_down)
    d_tokens, grad_gu, grad_dn = pl.pallas_call(
        finish_kernel,
        name="finish",
        out_shape=(jax.ShapeDtypeStruct((WIDTH, toks), BF16), *grads),
        in_specs=[hbm] * 4,
        out_specs=(vmem, hbm, hbm),
        scratch_shapes=[
            pltpu.VMEM((slots, toks), BF16),
            pltpu.VMEM((slots, PAD), BF16),
            pltpu.VMEM((SHARD, 2 * WIDTH), BF16),
            pltpu.VMEM((SHARD, WIDTH), BF16),
            pltpu.SemaphoreType.DMA((6,)),
        ],
        compiler_params=pltpu.CompilerParams(vmem_limit_bytes=60 * 2**20),
    )(pick, back.reshape(slots, PAD), grad_gu, grad_dn)
    return d_tokens.T, grad_gu[None], grad_dn[None]


def solution(mesh):
    in_specs = (
        P(("dp", "expert"), None),
        P(("dp", "expert"), None),
        P(("dp", "expert"), None),
        P(("dp", "expert"), None),
        P("expert", None, None),
        P("expert", None),
        P("expert", None, None),
    )
    out_specs = (P(("dp", "expert"), None), P("expert", "dp", None), P("expert", "dp", None))
    return jax.shard_map(shards, mesh=mesh, in_specs=in_specs, out_specs=out_specs, check_vma=False)
```

```python
import jax
import jax.numpy as jnp
from jax import lax
from jax.experimental import pallas as pl
from jax.experimental.pallas import tpu as pltpu
from jax.sharding import PartitionSpec as P

MESH = pl.DeviceIdType.MESH
F32 = jnp.float32
BF16 = jnp.bfloat16
OWNERS = 32
CAP = 24
WIDTH = 1440
MAIN = 1408
HALF = 720
SHARD = 360
LINES = 368
PAD = 1536
TILE = 512
PAGE = 256
GROUP = 8
ROWS = GROUP * CAP


def nt(a, b):
    return lax.dot_general(a, b, (((1,), (1,)), ((), ())), preferred_element_type=F32)


def tn(a, b):
    return lax.dot_general(a, b, (((0,), (0,)), ((), ())), preferred_element_type=F32)


def nn(a, b):
    return jnp.dot(a, b, preferred_element_type=F32)


def finish_kernel(
    tok_ref, gu_ref, dn_ref, out_tok_ref, out_gu_ref, out_dn_ref, tok, gu, dn, sem
):
    parts = (
        (gu_ref.at[:, 0:MAIN], gu.at[:, 0:MAIN], out_gu_ref.at[:, 0:MAIN]),
        (gu_ref.at[:, MAIN:], gu.at[:, MAIN:], out_gu_ref.at[:, MAIN:]),
        (dn_ref, dn, out_dn_ref),
        (tok_ref, tok, out_tok_ref),
    )
    ins = [pltpu.make_async_copy(a, b, sem.at[0, n]) for n, (a, b, _) in enumerate(parts)]
    outs = [pltpu.make_async_copy(b, c, sem.at[1, n]) for n, (_, b, c) in enumerate(parts)]
    for copy in ins:
        copy.start()
    for first, second in zip(ins, outs):
        first.wait()
        second.start()
    for copy in outs:
        copy.wait()


def main_kernel(
    ids_ref,
    probs_ref,
    bias_ref,
    tok_ref,
    dout_ref,
    wgu_ref,
    wdn_ref,
    out_tok_ref,
    out_gu_ref,
    out_dn_ref,
    back_ref,
    pick,
    page,
    out_gu,
    out_dn,
    tok,
    dout,
    code,
    prob,
    send,
    got,
    rows,
    scaled,
    wgu,
    wu,
    wdn,
    acc,
    work,
    rows_t,
    hid_t,
    give,
    take,
    load_sem,
    send_sem,
    recv_sem,
    fwd_send,
    fwd_recv,
    back_send,
    back_recv,
    self_sem,
    core_send,
    core_recv,
    page_sem,
    out_sem,
):
    dp = lax.axis_index("dp")
    me = lax.axis_index("expert")
    l = dp // 2
    c = dp % 2
    mx, mz, mh = me // 8, (me // 2) % 4, me % 2

    def target(r, sign):
        k, i, low = r // 8, (r // 2) % 4, r % 2
        x = (mx + sign * i + 4) % 4
        z = (mz + sign * (k - i) + 8) % 4
        h = (mh + low) % 2
        return (((l + low) % 2) * 2 + c, x * 8 + z * 2 + h)

    over_y = ((1 - l) * 2 + c, me)
    over_core = (l * 2 + 1 - c, me)

    loads = [
        pltpu.make_async_copy(src, dst, load_sem.at[n])
        for n, (src, dst) in enumerate(
            (
                (tok_ref, tok),
                (dout_ref, dout),
                (wgu_ref.at[0], wgu),
                (wdn_ref.at[0], wdn.at[pl.ds(0, WIDTH)]),
            )
        )
    ]
    for load in loads[:2]:
        load.start()

    barrier = pltpu.get_barrier_semaphore()

    def greet(r, _):
        pl.semaphore_signal(barrier, inc=1, device_id=target(r, 1), device_id_type=MESH)
        return 0

    lax.fori_loop(1, OWNERS, greet, 0)
    pl.semaphore_signal(barrier, inc=1, device_id=over_y, device_id_type=MESH)
    pl.semaphore_signal(barrier, inc=1, device_id=over_core, device_id_type=MESH)

    toks = ids_ref.shape[1]
    r = lax.broadcasted_iota(jnp.int32, (OWNERS, toks), 0)
    i = (r >> 1) & 3
    x = ((me >> 3) + i) & 3
    z = ((me >> 1) + (r >> 3) - i) & 3
    expert = x * 8 + z * 2 + ((me ^ r) & 1)
    named = jnp.zeros((OWNERS, toks), F32)
    weight = jnp.zeros((OWNERS, toks), F32)
    for k in range(ids_ref.shape[0]):
        hit = ids_ref[k : k + 1, :] == expert
        named = named + jnp.where(hit, 1.0, 0.0)
        weight = weight + jnp.where(hit, probs_ref[k : k + 1, :], 0.0)
    before = lax.broadcasted_iota(jnp.int32, (toks, toks), 0) < lax.broadcasted_iota(
        jnp.int32, (toks, toks), 1
    )
    rank = nn(named.astype(BF16), jnp.where(before, 1.0, 0.0).astype(BF16))
    code[...] = jnp.where(named > 0.0, rank, -1.0)
    prob[...] = weight
    for load in loads[:2]:
        load.wait()
    for load in loads[2:]:
        load.start()

    def fill(g):
        part = pl.ds(pl.multiple_of(g * GROUP, GROUP), GROUP)
        place = lax.broadcasted_iota(jnp.int32, (GROUP, CAP, toks), 1).astype(F32)
        chosen = jnp.broadcast_to(code[part, :][:, None, :], place.shape) == place
        ones = jnp.where(chosen, 1.0, 0.0).reshape(ROWS, toks).astype(BF16)
        share = jnp.where(chosen, jnp.broadcast_to(prob[part, :][:, None, :], place.shape), 0.0)
        share = jnp.sum(share, axis=2, keepdims=True).reshape(ROWS, 1)
        pick[pl.ds(pl.multiple_of(g * ROWS, ROWS), ROWS), :] = ones
        both = pl.ds(2 * g, 2)
        for n, src in enumerate((tok, dout)):
            value = nt(ones, src[...])
            if n == 1:
                value = value * share
            for first, last, where in (
                (0, MAIN, n * MAIN),
                (MAIN, WIDTH, 2 * MAIN + n * (WIDTH - MAIN)),
            ):
                piece = value[:, first:last].reshape(2, GROUP // 2, CAP, last - first)
                send[both, :, :, where : where + last - first] = piece.astype(BF16)

    def slot(region, r):
        return got.at[region, r // 4, r % 4]

    def relay_copy(src, dst, r, device):
        return pltpu.make_async_remote_copy(
            src_ref=src,
            dst_ref=dst,
            send_sem=fwd_send.at[r],
            recv_sem=fwd_recv.at[r],
            device_id=device,
            device_id_type=MESH,
        )

    def forward_block(r):
        return relay_copy(slot(0, r), slot(1, r), r, over_y)

    def dispatch(r, _):
        pltpu.make_async_remote_copy(
            src_ref=send.at[r // 4, r % 4],
            dst_ref=slot(0, r),
            send_sem=send_sem.at[r // 4],
            recv_sem=recv_sem.at[r],
            device_id=target(r, 1),
            device_id_type=MESH,
        ).start()
        return 0

    fill(0)
    pl.semaphore_wait(barrier, OWNERS + 1)
    own = pltpu.make_async_copy(send.at[0, 0], slot(0, 0), recv_sem.at[0])
    own.start()
    relay_copy(send.at[0, 0], slot(1, 0), 0, over_y).start()
    lax.fori_loop(1, GROUP, dispatch, 0)

    def fill_next(g, _):
        fill(g)
        lax.fori_loop(GROUP * g, GROUP * g + GROUP, dispatch, 0)
        return 0

    lax.fori_loop(1, OWNERS // GROUP, fill_next, 0)

    loads[2].wait()
    loads[3].wait()
    wdn[WIDTH:PAD, :] = jnp.zeros((PAD - WIDTH, WIDTH), BF16)
    wu[:, WIDTH:PAD] = jnp.zeros((WIDTH, PAD - WIDTH), BF16)

    def shift(q, _):
        lines = pl.ds(pl.multiple_of(q * 144, 16), 144)
        wu[lines, 0:WIDTH] = wgu[lines, WIDTH : 2 * WIDTH]
        return 0

    lax.fori_loop(0, 10, shift, 0)
    own.wait()

    def landed(r):
        pltpu.make_async_copy(slot(0, r), slot(0, r), recv_sem.at[r]).wait()

    def relay_block(r, _):
        landed(r)
        forward_block(r).start()
        return 0

    lax.fori_loop(1, GROUP, relay_block, 0)
    acc[...] = jnp.zeros_like(acc)

    def inner(region, first, count, start):
        size = count * (GROUP // 2) * CAP
        lines = slice(start, start + size)
        both = pl.ds(first, count)
        tail = 2 * MAIN
        more = WIDTH - MAIN
        for n, dst in enumerate((rows, scaled)):
            dst[lines, 0:MAIN] = got[region, both, :, :, n * MAIN : (n + 1) * MAIN].reshape(
                size, MAIN
            )
        ends = got[region, both, :, :, tail : tail + 2 * more].reshape(size, 2 * more)
        rows[lines, MAIN:WIDTH] = ends[:, 0:more]
        scaled[lines, MAIN:WIDTH] = ends[:, more:]
        for t in range(PAD // TILE):
            cols = slice(t * TILE, (t + 1) * TILE)
            bias_u = bias_ref[:, WIDTH + t * TILE : min(WIDTH + (t + 1) * TILE, 2 * WIDTH)]
            if bias_u.shape[1] < TILE:
                bias_u = jnp.concatenate(
                    [bias_u, jnp.zeros((1, TILE - bias_u.shape[1]), F32)], axis=1
                )
            g = nn(rows[lines, :], wgu[:, cols]) + bias_ref[:, cols]
            u = nn(rows[lines, :], wu[:, cols]) + bias_u + 1.0
            dh = nt(scaled[lines, :], wdn[cols, :])
            s = jax.nn.sigmoid(1.702 * g)
            glu = g * s
            work[2, lines, cols] = (u * glu).astype(BF16)
            work[1, lines, cols] = (dh * glu).astype(BF16)
            work[0, lines, cols] = (dh * u * (s + 1.702 * glu * (1.0 - s))).astype(BF16)

    def sent(p, count):
        some = send.at[p, pl.ds(4 - count, count)]
        pltpu.make_async_copy(some, some, send_sem.at[p]).wait()

    def back_copy(r):
        return pltpu.make_async_remote_copy(
            src_ref=send.at[r // 4, r % 4, :, pl.ds(0, PAD)],
            dst_ref=back_ref.at[r],
            send_sem=back_send,
            recv_sem=back_recv,
            device_id=target(r, -1),
            device_id_type=MESH,
        )

    own_back = pltpu.make_async_copy(
        send.at[0, 0, :, pl.ds(0, PAD)], back_ref.at[0], self_sem
    )

    def give_back(j):
        @pl.when(j == 0)
        def _():
            sent(0, 3)
            sent(1, 4)
            forward_block(0).wait_send()

        @pl.when(j > 0)
        def _():
            sent(2 * j, 4)
            sent(2 * j + 1, 4)

        for first in range(0, WIDTH, TILE):
            cols = slice(first, min(first + TILE, WIDTH))
            part = nt(work[0, 0:ROWS, :], wgu[cols, 0:PAD]) + nt(work[1, 0:ROWS, :], wu[cols, :])
            part = part.reshape(2, GROUP // 2, CAP, cols.stop - cols.start).astype(BF16)
            send[pl.ds(2 * j, 2), :, :, cols] = part

        def send_back(r, _):
            @pl.when(r == 0)
            def _():
                own_back.start()

            @pl.when(r > 0)
            def _():
                back_copy(r).start()

            return 0

        lax.fori_loop(GROUP * j, GROUP * j + GROUP, send_back, 0)

    def arrive(first, count):
        def one(r, _):
            forward_block(r).wait_recv()
            return 0

        lax.fori_loop(first, first + count, one, 0)

    def turn(lines):
        at = slice(0, lines.stop - lines.start)
        for side in range(2):

            @pl.when(l == side)
            def _():
                for q in range(2):
                    cols = slice(HALF * side + SHARD * q, HALF * side + SHARD * (q + 1))
                    rows_t[q, :, at] = rows[lines, cols].T
                    hid_t[q, :, at] = work[2, lines, cols].T

    def product(n, q, t, lines):
        left = (rows_t, rows_t, hid_t)[n][q, :, 0 : lines.stop - lines.start]
        cols = slice(t * TILE, (t + 1) * TILE)
        if n < 2:
            return cols, nn(left, work[n, lines, cols])
        cols = slice(t * TILE, min((t + 1) * TILE, WIDTH))
        return cols, nn(left, scaled[lines, cols])

    def add(lines):
        for n in range(3):
            for t in range(PAD // TILE):
                for q in range(2):
                    cols, value = product(n, q, t, lines)
                    acc[n, q, :, cols] += value

    every = slice(0, 2 * ROWS)

    def relay_group(g):
        lax.fori_loop(GROUP * g, GROUP * (g + 1), relay_block, 0)

    first = slice(0, ROWS)
    inner(0, 0, 2, 0)
    relay_group(1)
    give_back(0)
    turn(first)
    add(first)

    def superstep(j, _):
        @pl.when(j < 2)
        def _():
            relay_group(j + 2)

        inner(0, 2 * j + 2, 2, 0)
        give_back(j + 1)
        arrive(GROUP * j, GROUP)
        inner(1, 2 * j, 2, ROWS)
        turn(every)
        add(every)
        return 0

    lax.fori_loop(0, 3, superstep, 0)

    def outgoing(n):
        return give.at[n] if n < 2 else work.at[2, pl.ds(0, LINES)]

    def turn_page(t):
        cols = pl.ds(t * PAGE, PAGE)
        return pltpu.make_async_copy(back_ref.at[:, :, cols], page.at[t % 2], page_sem.at[t % 2])

    tok_out = pltpu.make_async_copy(tok, out_tok_ref, out_sem.at[3])

    def combine():
        some = back_ref.at[pl.ds(1, OWNERS - 1)]
        pltpu.make_async_copy(some, some, back_recv).wait()
        own_back.wait()
        turn_page(0).start()
        chosen = pick[...].T
        for t in range(PAD // PAGE):
            if t + 1 < PAD // PAGE:
                turn_page(t + 1).start()
            turn_page(t).wait()
            value = nn(chosen, page[t % 2].reshape(OWNERS * CAP, PAGE)).astype(BF16).T
            lines = slice(t * PAGE, min((t + 1) * PAGE, WIDTH))
            tok[lines, :] = value[0 : lines.stop - lines.start]
        tok_out.start()

    def core_copy(n):
        return pltpu.make_async_remote_copy(
            src_ref=outgoing(n),
            dst_ref=take.at[n],
            send_sem=core_send.at[n],
            recv_sem=core_recv.at[n],
            device_id=over_core,
            device_id_type=MESH,
        )

    late = slice(ROWS, 2 * ROWS)
    arrive(24, 4)
    inner(1, 6, 1, ROWS)
    arrive(28, 4)
    inner(1, 7, 1, ROWS + ROWS // 2)
    turn(late)
    for n in range(3):
        for t in range(PAD // TILE):
            cols, value = product(n, 1 - c, t, late)
            outgoing(n)[0:SHARD, cols] = (acc[n, 1 - c, :, cols] + value).astype(BF16)
        core_copy(n).start()
    combine()
    out_copies = (
        pltpu.make_async_copy(
            out_gu.at[:, 0:MAIN], out_gu_ref.at[:, 0:MAIN], out_sem.at[0]
        ),
        pltpu.make_async_copy(out_gu.at[:, MAIN:], out_gu_ref.at[:, MAIN:], out_sem.at[1]),
        pltpu.make_async_copy(out_dn, out_dn_ref, out_sem.at[2]),
    )
    for n in range(3):
        core_copy(n).wait_recv()
        for t in range(PAD // TILE):
            cols, value = product(n, c, t, late)
            cols = slice(cols.start, min(cols.stop, WIDTH))
            value = value[:, 0 : cols.stop - cols.start]
            total = acc[n, c, :, cols] + value + take[n, 0:SHARD, cols].astype(F32)
            if n < 2:
                out_gu[:, n * WIDTH + cols.start : n * WIDTH + cols.stop] = total.astype(BF16)
            else:
                out_dn[:, cols] = total.astype(BF16)
        out_copies[n].start()

    for n in range(3):
        core_copy(n).wait_send()

    def settle_block(r, _):
        forward_block(r).wait_send()
        return 0

    lax.fori_loop(1, OWNERS, settle_block, 0)
    some = back_ref.at[pl.ds(1, OWNERS - 1)]
    pltpu.make_async_copy(some, some, back_send).wait()
    for copy in (*out_copies, tok_out):
        copy.wait()


def shards(tokens, d_out, route_ids, route_probs, w_gate_up, gate_up_bias, w_down):
    toks = tokens.shape[0]
    vmem = pl.BlockSpec(memory_space=pltpu.VMEM)
    hbm = pl.BlockSpec(memory_space=pl.ANY)
    slots = OWNERS * CAP
    block = (CAP, 2 * WIDTH)
    results = (
        jax.ShapeDtypeStruct((WIDTH, toks), BF16),
        jax.ShapeDtypeStruct((SHARD, 2 * WIDTH), BF16),
        jax.ShapeDtypeStruct((SHARD, WIDTH), BF16),
    )
    d_tokens, grad_gu, grad_dn, _ = pl.pallas_call(
        main_kernel,
        name="experts",
        out_shape=(*results, jax.ShapeDtypeStruct((OWNERS, CAP, PAD), BF16)),
        in_specs=[vmem] * 3 + [hbm] * 4,
        out_specs=(hbm, hbm, hbm, hbm),
        scratch_shapes=[
            pltpu.VMEM((slots, toks), BF16),
            pltpu.VMEM((2, OWNERS, CAP, PAGE), BF16),
            pltpu.VMEM((SHARD, 2 * WIDTH), BF16),
            pltpu.VMEM((SHARD, WIDTH), BF16),
            pltpu.VMEM((WIDTH, toks), BF16),
            pltpu.VMEM((WIDTH, toks), BF16),
            pltpu.VMEM((OWNERS, toks), F32),
            pltpu.VMEM((OWNERS, toks), F32),
            pltpu.VMEM((8, 4, *block), BF16),
            pltpu.VMEM((2, 8, 4, *block), BF16),
            pltpu.VMEM((2 * ROWS, WIDTH), BF16),
            pltpu.VMEM((2 * ROWS, WIDTH), BF16),
            pltpu.VMEM((WIDTH, 2 * WIDTH), BF16),
            pltpu.VMEM((WIDTH, PAD), BF16),
            pltpu.VMEM((PAD, WIDTH), BF16),
            pltpu.VMEM((3, 2, SHARD, PAD), F32),
            pltpu.VMEM((3, 2 * ROWS, PAD), BF16),
            pltpu.VMEM((2, SHARD, 2 * ROWS), BF16),
            pltpu.VMEM((2, SHARD, 2 * ROWS), BF16),
            pltpu.VMEM((2, LINES, PAD), BF16),
            pltpu.VMEM((3, LINES, PAD), BF16),
            pltpu.SemaphoreType.DMA((4,)),
            pltpu.SemaphoreType.DMA((8,)),
            pltpu.SemaphoreType.DMA((OWNERS,)),
            pltpu.SemaphoreType.DMA((OWNERS,)),
            pltpu.SemaphoreType.DMA((OWNERS,)),
            pltpu.SemaphoreType.DMA,
            pltpu.SemaphoreType.DMA,
            pltpu.SemaphoreType.DMA,
            pltpu.SemaphoreType.DMA((3,)),
            pltpu.SemaphoreType.DMA((3,)),
            pltpu.SemaphoreType.DMA((2,)),
            pltpu.SemaphoreType.DMA((4,)),
        ],
        compiler_params=pltpu.CompilerParams(
            collective_id=0, has_side_effects=True, vmem_limit_bytes=638 * 2**20 // 10
        ),
    )(route_ids.T, route_probs.T, gate_up_bias, tokens.T, d_out.T, w_gate_up, w_down)
    d_tokens, grad_gu, grad_dn = pl.pallas_call(
        finish_kernel,
        name="finish",
        out_shape=results,
        in_specs=[hbm] * 3,
        out_specs=(hbm, hbm, hbm),
        scratch_shapes=[
            *(pltpu.VMEM(result.shape, BF16) for result in results),
            pltpu.SemaphoreType.DMA((2, 4)),
        ],
        compiler_params=pltpu.CompilerParams(vmem_limit_bytes=60 * 2**20),
    )(d_tokens, grad_gu, grad_dn)
    return d_tokens.T, grad_gu[None], grad_dn[None]


def solution(mesh):
    in_specs = (
        P(("dp", "expert"), None),
        P(("dp", "expert"), None),
        P(("dp", "expert"), None),
        P(("dp", "expert"), None),
        P("expert", None, None),
        P("expert", None),
        P("expert", None, None),
    )
    out_specs = (P(("dp", "expert"), None), P("expert", "dp", None), P("expert", "dp", None))
    return jax.shard_map(shards, mesh=mesh, in_specs=in_specs, out_specs=out_specs, check_vma=False)
```

```python
import jax
import jax.numpy as jnp
from jax import lax
from jax.experimental import pallas as pl
from jax.experimental.pallas import tpu as pltpu
from jax.sharding import PartitionSpec as P

MESH = pl.DeviceIdType.MESH
F32 = jnp.float32
BF16 = jnp.bfloat16
OWNERS = 32
CAP = 24
WIDTH = 1440
MAIN = 1408
HALF = 720
SHARD = 360
LINES = 368
PAD = 1536
TILE = 512
GROUP = 8
ROWS = GROUP * CAP


def nt(a, b):
    return lax.dot_general(a, b, (((1,), (1,)), ((), ())), preferred_element_type=F32)


def tn(a, b):
    return lax.dot_general(a, b, (((0,), (0,)), ((), ())), preferred_element_type=F32)


def nn(a, b):
    return jnp.dot(a, b, preferred_element_type=F32)


def finish_kernel(
    tok_ref, gu_ref, dn_ref, out_tok_ref, out_gu_ref, out_dn_ref, tok, gu, dn, sem
):
    parts = (
        (gu_ref.at[:, 0:MAIN], gu.at[:, 0:MAIN], out_gu_ref.at[:, 0:MAIN]),
        (gu_ref.at[:, MAIN:], gu.at[:, MAIN:], out_gu_ref.at[:, MAIN:]),
        (dn_ref, dn, out_dn_ref),
        (tok_ref, tok, out_tok_ref),
    )
    ins = [pltpu.make_async_copy(a, b, sem.at[0, n]) for n, (a, b, _) in enumerate(parts)]
    outs = [pltpu.make_async_copy(b, c, sem.at[1, n]) for n, (_, b, c) in enumerate(parts)]
    for copy in ins:
        copy.start()
    for first, second in zip(ins, outs):
        first.wait()
        second.start()
    for copy in outs:
        copy.wait()


def main_kernel(
    ids_ref,
    probs_ref,
    bias_ref,
    tok_ref,
    dout_ref,
    wgu_ref,
    wdn_ref,
    out_tok_ref,
    out_gu_ref,
    out_dn_ref,
    back_ref,
    pick,
    out_gu,
    out_dn,
    tok,
    dout,
    code,
    prob,
    send,
    got,
    rows,
    scaled,
    wgu,
    wu,
    wdn,
    acc,
    work,
    rows_t,
    hid_t,
    give,
    take,
    load_sem,
    send_sem,
    recv_sem,
    fwd_send,
    fwd_recv,
    back_send,
    back_recv,
    self_sem,
    core_send,
    core_recv,
    page_sem,
    out_sem,
):
    dp = lax.axis_index("dp")
    me = lax.axis_index("expert")
    l = dp // 2
    c = dp % 2
    mx, mz, mh = me // 8, (me // 2) % 4, me % 2

    def target(r, sign):
        k, i, low = r // 8, (r // 2) % 4, r % 2
        x = (mx + sign * i + 4) % 4
        z = (mz + sign * (k - i) + 8) % 4
        h = (mh + low) % 2
        return (((l + low) % 2) * 2 + c, x * 8 + z * 2 + h)

    over_y = ((1 - l) * 2 + c, me)
    over_core = (l * 2 + 1 - c, me)

    loads = [
        pltpu.make_async_copy(src, dst, load_sem.at[n])
        for n, (src, dst) in enumerate(
            (
                (tok_ref, tok),
                (dout_ref, dout),
                (wgu_ref.at[0], wgu),
                (wdn_ref.at[0], wdn.at[pl.ds(0, WIDTH)]),
            )
        )
    ]
    for load in loads[:2]:
        load.start()

    barrier = pltpu.get_barrier_semaphore()

    def greet(r, _):
        pl.semaphore_signal(barrier, inc=1, device_id=target(r, 1), device_id_type=MESH)
        return 0

    lax.fori_loop(1, OWNERS, greet, 0)
    pl.semaphore_signal(barrier, inc=1, device_id=over_y, device_id_type=MESH)
    pl.semaphore_signal(barrier, inc=1, device_id=over_core, device_id_type=MESH)

    toks = ids_ref.shape[1]
    r = lax.broadcasted_iota(jnp.int32, (OWNERS, toks), 0)
    i = (r >> 1) & 3
    x = ((me >> 3) + i) & 3
    z = ((me >> 1) + (r >> 3) - i) & 3
    expert = x * 8 + z * 2 + ((me ^ r) & 1)
    named = jnp.zeros((OWNERS, toks), F32)
    weight = jnp.zeros((OWNERS, toks), F32)
    for k in range(ids_ref.shape[0]):
        hit = ids_ref[k : k + 1, :] == expert
        named = named + jnp.where(hit, 1.0, 0.0)
        weight = weight + jnp.where(hit, probs_ref[k : k + 1, :], 0.0)
    before = lax.broadcasted_iota(jnp.int32, (toks, toks), 0) < lax.broadcasted_iota(
        jnp.int32, (toks, toks), 1
    )
    rank = nn(named.astype(BF16), jnp.where(before, 1.0, 0.0).astype(BF16))
    code[...] = jnp.where(named > 0.0, rank, -1.0)
    prob[...] = weight
    for load in loads[:2]:
        load.wait()
    for load in loads[2:]:
        load.start()

    def fill(g):
        part = pl.ds(pl.multiple_of(g * GROUP, GROUP), GROUP)
        place = lax.broadcasted_iota(jnp.int32, (GROUP, CAP, toks), 1).astype(F32)
        chosen = jnp.broadcast_to(code[part, :][:, None, :], place.shape) == place
        ones = jnp.where(chosen, 1.0, 0.0).reshape(ROWS, toks).astype(BF16)
        share = jnp.where(chosen, jnp.broadcast_to(prob[part, :][:, None, :], place.shape), 0.0)
        share = jnp.sum(share, axis=2, keepdims=True).reshape(ROWS, 1)
        pick[pl.ds(pl.multiple_of(g * ROWS, ROWS), ROWS), :] = ones
        both = pl.ds(2 * g, 2)
        for n, src in enumerate((tok, dout)):
            value = nt(ones, src[...])
            if n == 1:
                value = value * share
            for first, last, where in (
                (0, MAIN, n * MAIN),
                (MAIN, WIDTH, 2 * MAIN + n * (WIDTH - MAIN)),
            ):
                piece = value[:, first:last].reshape(2, GROUP // 2, CAP, last - first)
                send[both, :, :, where : where + last - first] = piece.astype(BF16)

    def slot(region, r):
        return got.at[region, r // 4, r % 4]

    def relay_copy(src, dst, r, device):
        return pltpu.make_async_remote_copy(
            src_ref=src,
            dst_ref=dst,
            send_sem=fwd_send.at[r],
            recv_sem=fwd_recv.at[r],
            device_id=device,
            device_id_type=MESH,
        )

    def forward_block(r):
        return relay_copy(slot(0, r), slot(1, r), r, over_y)

    def dispatch(r, _):
        pltpu.make_async_remote_copy(
            src_ref=send.at[r // 4, r % 4],
            dst_ref=slot(0, r),
            send_sem=send_sem.at[r // 4],
            recv_sem=recv_sem.at[r],
            device_id=target(r, 1),
            device_id_type=MESH,
        ).start()
        return 0

    fill(0)
    pl.semaphore_wait(barrier, OWNERS + 1)
    own = pltpu.make_async_copy(send.at[0, 0], slot(0, 0), recv_sem.at[0])
    own.start()
    relay_copy(send.at[0, 0], slot(1, 0), 0, over_y).start()
    lax.fori_loop(1, GROUP, dispatch, 0)

    def landed(r):
        pltpu.make_async_copy(slot(0, r), slot(0, r), recv_sem.at[r]).wait()

    def relay_block(r, _):
        landed(r)
        forward_block(r).start()
        return 0

    def fill_next(g, _):
        fill(g)
        lax.fori_loop(GROUP * g, GROUP * g + GROUP, dispatch, 0)
        return relay_block(g, 0)

    lax.fori_loop(1, OWNERS // GROUP, fill_next, 0)
    lax.fori_loop(OWNERS // GROUP, GROUP - 2, relay_block, 0)

    loads[2].wait()
    loads[3].wait()
    wdn[WIDTH:PAD, :] = jnp.zeros((PAD - WIDTH, WIDTH), BF16)
    wu[:, WIDTH:PAD] = jnp.zeros((WIDTH, PAD - WIDTH), BF16)

    def shift(q, _):
        lines = pl.ds(pl.multiple_of(q * 144, 16), 144)
        wu[lines, 0:WIDTH] = wgu[lines, WIDTH : 2 * WIDTH]
        return 0

    lax.fori_loop(0, 10, shift, 0)
    own.wait()

    lax.fori_loop(GROUP - 2, GROUP, relay_block, 0)
    acc[...] = jnp.zeros_like(acc)

    def inner(region, first, count, start):
        size = count * (GROUP // 2) * CAP
        lines = slice(start, start + size)
        both = pl.ds(first, count)
        tail = 2 * MAIN
        more = WIDTH - MAIN
        for n, dst in enumerate((rows, scaled)):
            dst[lines, 0:MAIN] = got[region, both, :, :, n * MAIN : (n + 1) * MAIN].reshape(
                size, MAIN
            )
        ends = got[region, both, :, :, tail : tail + 2 * more].reshape(size, 2 * more)
        rows[lines, MAIN:WIDTH] = ends[:, 0:more]
        scaled[lines, MAIN:WIDTH] = ends[:, more:]
        for t in range(PAD // TILE):
            cols = slice(t * TILE, (t + 1) * TILE)
            bias_u = bias_ref[:, WIDTH + t * TILE : min(WIDTH + (t + 1) * TILE, 2 * WIDTH)]
            if bias_u.shape[1] < TILE:
                bias_u = jnp.concatenate(
                    [bias_u, jnp.zeros((1, TILE - bias_u.shape[1]), F32)], axis=1
                )
            g = nn(rows[lines, :], wgu[:, cols]) + bias_ref[:, cols]
            u = nn(rows[lines, :], wu[:, cols]) + bias_u + 1.0
            dh = nt(scaled[lines, :], wdn[cols, :])
            s = jax.nn.sigmoid(1.702 * g)
            glu = g * s
            work[2, lines, cols] = (u * glu).astype(BF16)
            work[1, lines, cols] = (dh * glu).astype(BF16)
            work[0, lines, cols] = (dh * u * (s + 1.702 * glu * (1.0 - s))).astype(BF16)

    def sent(p, count):
        some = send.at[p, pl.ds(4 - count, count)]
        pltpu.make_async_copy(some, some, send_sem.at[p]).wait()

    def back_copy(r):
        return pltpu.make_async_remote_copy(
            src_ref=send.at[r // 4, r % 4, :, pl.ds(0, PAD)],
            dst_ref=back_ref.at[r],
            send_sem=back_send,
            recv_sem=back_recv,
            device_id=target(r, -1),
            device_id_type=MESH,
        )

    own_back = pltpu.make_async_copy(
        send.at[0, 0, :, pl.ds(0, PAD)], back_ref.at[0], self_sem
    )

    def give_back(j):
        @pl.when(j == 0)
        def _():
            sent(0, 3)
            sent(1, 4)
            forward_block(0).wait_send()

        @pl.when(j > 0)
        def _():
            sent(2 * j, 4)
            sent(2 * j + 1, 4)

        for first in range(0, WIDTH, TILE):
            cols = slice(first, min(first + TILE, WIDTH))
            part = nt(work[0, 0:ROWS, :], wgu[cols, 0:PAD]) + nt(work[1, 0:ROWS, :], wu[cols, :])
            part = part.reshape(2, GROUP // 2, CAP, cols.stop - cols.start).astype(BF16)
            send[pl.ds(2 * j, 2), :, :, cols] = part

        def send_back(r, _):
            @pl.when(r == 0)
            def _():
                own_back.start()

            @pl.when(r > 0)
            def _():
                back_copy(r).start()

            return 0

        lax.fori_loop(GROUP * j, GROUP * j + GROUP, send_back, 0)

    def arrive(first, count):
        def one(r, _):
            forward_block(r).wait_recv()
            return 0

        lax.fori_loop(first, first + count, one, 0)

    def turn(lines):
        at = slice(0, lines.stop - lines.start)
        for side in range(2):

            @pl.when(l == side)
            def _():
                for q in range(2):
                    cols = slice(HALF * side + SHARD * q, HALF * side + SHARD * (q + 1))
                    rows_t[q, :, at] = rows[lines, cols].T
                    hid_t[q, :, at] = work[2, lines, cols].T

    def product(n, q, t, lines):
        left = (rows_t, rows_t, hid_t)[n][q, :, 0 : lines.stop - lines.start]
        cols = slice(t * TILE, (t + 1) * TILE)
        if n < 2:
            return cols, nn(left, work[n, lines, cols])
        cols = slice(t * TILE, min((t + 1) * TILE, WIDTH))
        return cols, nn(left, scaled[lines, cols])

    def add(lines):
        for n in range(3):
            for t in range(PAD // TILE):
                for q in range(2):
                    cols, value = product(n, q, t, lines)
                    acc[n, q, :, cols] += value

    every = slice(0, 2 * ROWS)

    def relay_group(g):
        lax.fori_loop(GROUP * g, GROUP * (g + 1), relay_block, 0)

    first = slice(0, ROWS)
    inner(0, 0, 2, 0)
    relay_group(1)
    give_back(0)
    turn(first)
    add(first)

    def superstep(j, _):
        @pl.when(j < 2)
        def _():
            relay_group(j + 2)

        inner(0, 2 * j + 2, 2, 0)
        give_back(j + 1)
        arrive(GROUP * j, GROUP)
        inner(1, 2 * j, 2, ROWS)
        turn(every)
        add(every)
        return 0

    lax.fori_loop(0, 3, superstep, 0)

    def outgoing(n):
        return give.at[n] if n < 2 else work.at[2, pl.ds(0, LINES)]

    def returned(p):
        return pltpu.make_async_copy(
            back_ref.at[pl.ds(4 * p, 4)], got.at[0, p, :, :, pl.ds(0, PAD)], page_sem.at[p]
        )

    def fetch(p, _):
        returned(p).start()
        return 0

    def settle(r, _):
        forward_block(r).wait_send()
        return 0

    tok_out = pltpu.make_async_copy(tok, out_tok_ref, out_sem.at[3])

    def combine():
        for p in range(8):
            returned(p).wait()
        chosen = pick[...].T
        for t in range(PAD // TILE):
            cols = slice(t * TILE, min((t + 1) * TILE, WIDTH))
            page = got[0, :, :, :, cols].reshape(OWNERS * CAP, cols.stop - cols.start)
            tok[cols, :] = nn(chosen, page).astype(BF16).T
        tok_out.start()

    def core_copy(n):
        return pltpu.make_async_remote_copy(
            src_ref=outgoing(n),
            dst_ref=take.at[n],
            send_sem=core_send.at[n],
            recv_sem=core_recv.at[n],
            device_id=over_core,
            device_id_type=MESH,
        )

    late = slice(ROWS, 2 * ROWS)
    arrive(24, 4)
    inner(1, 6, 1, ROWS)
    arrive(28, 4)
    inner(1, 7, 1, ROWS + ROWS // 2)
    lax.fori_loop(1, OWNERS, settle, 0)
    some = back_ref.at[pl.ds(1, OWNERS - 1)]
    pltpu.make_async_copy(some, some, back_recv).wait()
    own_back.wait()
    lax.fori_loop(0, 8, fetch, 0)
    turn(late)
    for n in range(3):
        for t in range(PAD // TILE):
            cols, value = product(n, 1 - c, t, late)
            outgoing(n)[0:SHARD, cols] = (acc[n, 1 - c, :, cols] + value).astype(BF16)
        core_copy(n).start()
    combine()
    out_copies = (
        pltpu.make_async_copy(
            out_gu.at[:, 0:MAIN], out_gu_ref.at[:, 0:MAIN], out_sem.at[0]
        ),
        pltpu.make_async_copy(out_gu.at[:, MAIN:], out_gu_ref.at[:, MAIN:], out_sem.at[1]),
        pltpu.make_async_copy(out_dn, out_dn_ref, out_sem.at[2]),
    )
    for n in range(3):
        core_copy(n).wait_recv()
        for t in range(PAD // TILE):
            cols, value = product(n, c, t, late)
            cols = slice(cols.start, min(cols.stop, WIDTH))
            value = value[:, 0 : cols.stop - cols.start]
            total = acc[n, c, :, cols] + value + take[n, 0:SHARD, cols].astype(F32)
            if n < 2:
                out_gu[:, n * WIDTH + cols.start : n * WIDTH + cols.stop] = total.astype(BF16)
            else:
                out_dn[:, cols] = total.astype(BF16)
        out_copies[n].start()

    for n in range(3):
        core_copy(n).wait_send()

    some = back_ref.at[pl.ds(1, OWNERS - 1)]
    pltpu.make_async_copy(some, some, back_send).wait()
    for copy in (*out_copies, tok_out):
        copy.wait()


def shards(tokens, d_out, route_ids, route_probs, w_gate_up, gate_up_bias, w_down):
    toks = tokens.shape[0]
    vmem = pl.BlockSpec(memory_space=pltpu.VMEM)
    hbm = pl.BlockSpec(memory_space=pl.ANY)
    slots = OWNERS * CAP
    block = (CAP, 2 * WIDTH)
    results = (
        jax.ShapeDtypeStruct((WIDTH, toks), BF16),
        jax.ShapeDtypeStruct((SHARD, 2 * WIDTH), BF16),
        jax.ShapeDtypeStruct((SHARD, WIDTH), BF16),
    )
    d_tokens, grad_gu, grad_dn, _ = pl.pallas_call(
        main_kernel,
        name="experts",
        out_shape=(*results, jax.ShapeDtypeStruct((OWNERS, CAP, PAD), BF16)),
        in_specs=[vmem] * 3 + [hbm] * 4,
        out_specs=(hbm, hbm, hbm, hbm),
        scratch_shapes=[
            pltpu.VMEM((slots, toks), BF16),
            pltpu.VMEM((SHARD, 2 * WIDTH), BF16),
            pltpu.VMEM((SHARD, WIDTH), BF16),
            pltpu.VMEM((WIDTH, toks), BF16),
            pltpu.VMEM((WIDTH, toks), BF16),
            pltpu.VMEM((OWNERS, toks), F32),
            pltpu.VMEM((OWNERS, toks), F32),
            pltpu.VMEM((8, 4, *block), BF16),
            pltpu.VMEM((2, 8, 4, *block), BF16),
            pltpu.VMEM((2 * ROWS, WIDTH), BF16),
            pltpu.VMEM((2 * ROWS, WIDTH), BF16),
            pltpu.VMEM((WIDTH, 2 * WIDTH), BF16),
            pltpu.VMEM((WIDTH, PAD), BF16),
            pltpu.VMEM((PAD, WIDTH), BF16),
            pltpu.VMEM((3, 2, SHARD, PAD), F32),
            pltpu.VMEM((3, 2 * ROWS, PAD), BF16),
            pltpu.VMEM((2, SHARD, 2 * ROWS), BF16),
            pltpu.VMEM((2, SHARD, 2 * ROWS), BF16),
            pltpu.VMEM((2, LINES, PAD), BF16),
            pltpu.VMEM((3, LINES, PAD), BF16),
            pltpu.SemaphoreType.DMA((4,)),
            pltpu.SemaphoreType.DMA((8,)),
            pltpu.SemaphoreType.DMA((OWNERS,)),
            pltpu.SemaphoreType.DMA((OWNERS,)),
            pltpu.SemaphoreType.DMA((OWNERS,)),
            pltpu.SemaphoreType.DMA,
            pltpu.SemaphoreType.DMA,
            pltpu.SemaphoreType.DMA,
            pltpu.SemaphoreType.DMA((3,)),
            pltpu.SemaphoreType.DMA((3,)),
            pltpu.SemaphoreType.DMA((8,)),
            pltpu.SemaphoreType.DMA((4,)),
        ],
        compiler_params=pltpu.CompilerParams(
            collective_id=0, has_side_effects=True, vmem_limit_bytes=638 * 2**20 // 10
        ),
    )(route_ids.T, route_probs.T, gate_up_bias, tokens.T, d_out.T, w_gate_up, w_down)
    d_tokens, grad_gu, grad_dn = pl.pallas_call(
        finish_kernel,
        name="finish",
        out_shape=results,
        in_specs=[hbm] * 3,
        out_specs=(hbm, hbm, hbm),
        scratch_shapes=[
            *(pltpu.VMEM(result.shape, BF16) for result in results),
            pltpu.SemaphoreType.DMA((2, 4)),
        ],
        compiler_params=pltpu.CompilerParams(vmem_limit_bytes=60 * 2**20),
    )(d_tokens, grad_gu, grad_dn)
    return d_tokens.T, grad_gu[None], grad_dn[None]


def solution(mesh):
    in_specs = (
        P(("dp", "expert"), None),
        P(("dp", "expert"), None),
        P(("dp", "expert"), None),
        P(("dp", "expert"), None),
        P("expert", None, None),
        P("expert", None),
        P("expert", None, None),
    )
    out_specs = (P(("dp", "expert"), None), P("expert", "dp", None), P("expert", "dp", None))
    return jax.shard_map(shards, mesh=mesh, in_specs=in_specs, out_specs=out_specs, check_vma=False)
```
